32 devices in a mesh: tm: 4 (over x, core), band: 8 (over z, y).
Axes of the slice: x: 2, y: 2, z: 4, core: 2. Of those that a mesh axis runs over, the one named last changes fastest.
Arguments:
- volts: bfloat16 [2, 1024, 262144], P(None, 'band', 'tm'), may hold values from -4 to 4
- taps: float32 [8, 256], replicated, may hold values from -2 to 2
Outputs:
- visibilities: float32 [256, 2, 1024, 1024], P(('tm', 'band'))
The draws below stay inside these ranges and needn't reach their ends.
All inputs are finite; a program needn't handle non-finite values.
Results may differ from the reference program's by a relative error of at most 0.0046.
Values may be sent and summed in bfloat16 or wider, within the bound.
A program may use at most 256 MiB of HBM per device.

```python
import math
import jax
import jax.numpy as jnp
from jax import lax

INPUTS = 1024
CHANNELS = 256
TAPS = 8
SPECTRA = 1024
SAMPLES = 262144


def block_levels(rng, dims, shards, low, high):
    def one(axis_at, blocks):
        steps = jax.random.uniform(jax.random.fold_in(jax.random.fold_in(rng, 6), axis_at), (blocks,), jnp.float32, low / len(shards), high / len(shards))
        return jnp.repeat(jnp.exp(steps), dims[axis_at] // blocks).reshape((-1,) + (1,) * (len(dims) - axis_at - 1))

    gain = one(*shards[0])
    for cut in shards[1:]:
        gain = gain * one(*cut)
    return gain


def bell_draw(own_key, dims, width, reach, cuts=(), kind=jnp.bfloat16):
    array = jax.random.normal(own_key, dims, jnp.float32) * width
    if len(cuts) > 0:
        array = block_levels(own_key, dims, cuts, -0.22, 0.18) * array
    return jnp.clip(array, min=-reach, max=reach).astype(kind)


def setup_inputs(seed: int = 0) -> dict:
    keys = jax.random.split(jax.random.key(seed), 3)
    volts = bell_draw(keys[0], (2, INPUTS, SAMPLES), 1.0, 4.0, ((1, 8), (2, 4)))
    taps = bell_draw(keys[1], (TAPS, CHANNELS), 0.5, 2.0, (), jnp.float32)
    return {"volts": volts, "taps": taps}


def dft_table():
    index = jnp.arange(CHANNELS, dtype=jnp.int32)
    turns = index[:, None] * index[None, :] % CHANNELS
    theta = turns.astype(jnp.float32) * (2.0 * math.pi / CHANNELS)
    factor = 1.0 / math.sqrt(CHANNELS)
    cosine = jnp.cos(theta) * factor
    sine = jnp.sin(theta) * factor
    real_row = jnp.stack([cosine, sine], axis=1)
    imag_row = jnp.stack([-sine, cosine], axis=1)
    table = jnp.stack([real_row, imag_row], axis=1)
    return table.reshape(2 * CHANNELS, 2, CHANNELS).astype(jnp.bfloat16)

def block_spectra(group_volts, taps, table):
    count = group_volts.shape[1]
    leading = jnp.zeros((2, count, (TAPS - 1) * CHANNELS), group_volts.dtype)
    frames = jnp.concatenate([leading, group_volts], axis=2)
    frames = frames.reshape(2, count, SPECTRA + TAPS - 1, CHANNELS).astype(jnp.float32)
    filtered = taps[0] * frames[:, :, 0:SPECTRA, :]
    for weight_index in range(1, TAPS):
        filtered = filtered + taps[weight_index] * frames[:, :, weight_index:weight_index + SPECTRA, :]
    filtered = filtered.astype(jnp.bfloat16)
    spectra = jnp.einsum('mrk,rnsk->mns', table.astype(jnp.float32), filtered.astype(jnp.float32), precision=lax.Precision.HIGHEST)
    return spectra.astype(jnp.bfloat16).reshape(CHANNELS, 2, count, SPECTRA)

def one_channel(signal):
    signal = signal.astype(jnp.float32)
    swapped = jnp.stack([signal[1], -signal[0]])
    weight = jnp.stack([signal, swapped])
    products = jnp.einsum('orps,rqs->opq', weight, signal, precision=lax.Precision.HIGHEST)
    return products * (1.0 / SPECTRA)

def reference(volts, taps):
    table = dft_table()
    group_size = 64
    grouped = volts.reshape(2, INPUTS // group_size, group_size, SAMPLES).transpose(1, 0, 2, 3)
    per_group = lax.map(lambda group_volts: block_spectra(group_volts, taps, table), grouped)
    spectra = per_group.transpose(1, 2, 0, 3, 4).reshape(CHANNELS, 2, INPUTS, SPECTRA)
    return lax.map(one_channel, spectra)
```

```python
import functools
import math

import jax
import jax.numpy as jnp
from jax import lax
from jax.experimental import pallas as pl
from jax.experimental.pallas import tpu as pltpu
from jax.sharding import PartitionSpec as P


def shifted(shard, axis, by):
    size = lax.axis_size(axis)
    pairs = [(i, i + by) for i in range(size) if 0 <= i + by < size]
    return lax.ppermute(shard, axis, pairs)


def dft_table(channels):
    index = jnp.arange(channels, dtype=jnp.int32)
    turns = index[:, None] * index[None, :] % channels
    theta = turns.astype(jnp.float32) * (2.0 * math.pi / channels)
    factor = 1.0 / math.sqrt(channels)
    cosine = jnp.cos(theta) * factor
    sine = jnp.sin(theta) * factor
    real_row = jnp.stack([cosine, sine], axis=1)
    imag_row = jnp.stack([-sine, cosine], axis=1)
    table = jnp.stack([real_row, imag_row], axis=1)
    return table.reshape(2 * channels, 2, channels).astype(jnp.bfloat16)


def weighting(signal):
    swapped = jnp.stack([signal[:, 1], -signal[:, 0]], axis=1)
    return jnp.stack([signal, swapped], axis=1)


def square_products(signal):
    return jnp.einsum(
        "corps,crqs->copq", weighting(signal), signal, preferred_element_type=jnp.float32
    )


def correlate(signal):
    return square_products(signal)


STEP = 16
STRIP = 16
LANES = 128
BLOCK = 256
MESH = pl.DeviceIdType.MESH


def filter_block(volts_ref, history_ref, taps_ref, filtered_ref, steps):
    taps_count, channels = taps_ref.shape
    inputs = history_ref.shape[1]
    margin = taps_count - 1

    def strip(index, carry):
        rows = pl.ds(pl.multiple_of(index * STRIP, STRIP), STRIP)
        for part in range(2):
            for lane in range(0, channels, LANES):
                weights = [
                    jnp.broadcast_to(taps_ref[j : j + 1, lane : lane + LANES], (STRIP, LANES))
                    for j in range(taps_count)
                ]
                frames = []
                for f in range(steps + margin):
                    ref, at = (history_ref, f) if f < margin else (volts_ref, f - margin)
                    start = at * channels + lane
                    frames.append(ref[part, rows, start : start + LANES].astype(jnp.float32))
                for t in range(steps):
                    total = weights[0] * frames[t]
                    for j in range(1, taps_count):
                        total = total + weights[j] * frames[t + j]
                    out_rows = pl.ds(pl.multiple_of(t * inputs + index * STRIP, STRIP), STRIP)
                    column = part * channels + lane
                    filtered_ref[out_rows, column : column + LANES] = total.astype(jnp.bfloat16)
        return carry

    lax.fori_loop(0, inputs // STRIP, strip, 0)


def transform_block(table_ref, filtered_ref, turned_ref, steps, inputs):
    rows = table_ref.shape[0]
    for t in range(0, steps, 2):
        product = lax.dot_general(
            table_ref[...],
            filtered_ref[t * inputs : (t + 2) * inputs, :],
            (((1,), (1,)), ((), ())),
            preferred_element_type=jnp.float32,
        )
        turned_ref[pl.ds(t, rows, stride=steps), :] = product[:, :inputs]
        turned_ref[pl.ds(t + 1, rows, stride=steps), :] = product[:, inputs:]


def exchange_kernel(
    groups,
    volts_ref,
    history_in_ref,
    taps_ref,
    table_ref,
    arrived_ref,
    volts_buf,
    history,
    filtered,
    turned,
    spectra,
    in_sem,
    send_sem,
    recv_sem,
    local_sem,
):
    time_groups, band_groups = groups
    devices = time_groups * band_groups
    my_time = lax.axis_index("tm")
    my_band = lax.axis_index("band")
    me = my_time * band_groups + my_band
    blocks, _, planes, steps, inputs = spectra.shape
    channels = taps_ref.shape[1]
    width = steps * channels

    def offset(k):
        turn = lax.rem(k, band_groups)
        half = turn // 2
        parity = lax.rem(turn, 2)
        by_band = lax.rem(band_groups // 2 + half + parity * (band_groups // 2), band_groups)
        by_time = lax.rem(k // band_groups + turn, time_groups)
        return by_time, by_band

    def fetch(block):
        slot = lax.rem(block, 2)
        columns = pl.ds(pl.multiple_of(block * width, LANES), width)
        return pltpu.make_async_copy(
            volts_ref.at[:, :, columns], volts_buf.at[slot], in_sem.at[slot]
        )

    fetch(0).start()
    history[...] = history_in_ref[...]

    barrier = pltpu.get_barrier_semaphore()

    def greet(k, carry):
        there_time = lax.rem(my_time + k // band_groups, time_groups)
        there_band = lax.rem(my_band + lax.rem(k, band_groups), band_groups)
        pl.semaphore_signal(
            barrier, inc=1, device_id=(there_time, there_band), device_id_type=MESH
        )
        return carry

    lax.fori_loop(1, devices, greet, 0)
    pl.semaphore_wait(barrier, devices - 1)

    def step(block, carry):
        slot = lax.rem(block, 2)
        fetch(block).wait()

        @pl.when(block + 1 < blocks)
        def _():
            fetch(block + 1).start()

        filter_block(volts_buf.at[slot], history, taps_ref, filtered, steps)
        margin = history.shape[2]
        history[...] = volts_buf[slot, :, :, width - margin :]
        transform_block(table_ref, filtered, turned, steps, inputs)

        def pack(there, carry):
            rows = pl.ds(pl.multiple_of(there * (planes * steps), STRIP), planes * steps)
            values = turned[rows, :].reshape(planes, steps, inputs)
            spectra[block, there] = values.astype(jnp.bfloat16)
            return carry

        lax.fori_loop(0, devices, pack, 0)

        def send(k, carry):
            by_time, by_band = offset(k)
            there_time = lax.rem(my_time + by_time, time_groups)
            there_band = lax.rem(my_band + by_band, band_groups)
            there = there_time * band_groups + there_band

            @pl.when(there != me)
            def _():
                pltpu.make_async_remote_copy(
                    src_ref=spectra.at[block, there],
                    dst_ref=arrived_ref.at[me, block],
                    send_sem=send_sem.at[there],
                    recv_sem=recv_sem.at[me],
                    device_id=(there_time, there_band),
                    device_id_type=MESH,
                ).start()

            return carry

        lax.fori_loop(0, devices, send, 0)
        return carry

    lax.fori_loop(0, blocks, step, 0)
    own = pltpu.make_async_copy(spectra.at[:, me], arrived_ref.at[me], local_sem)
    own.start()

    def finish(k, carry):
        there_time = lax.rem(my_time + k // band_groups, time_groups)
        there_band = lax.rem(my_band + lax.rem(k, band_groups), band_groups)
        there = there_time * band_groups + there_band
        pltpu.make_async_copy(spectra.at[:, there], arrived_ref.at[there], send_sem.at[there]).wait()
        pltpu.make_async_copy(spectra.at[:, there], arrived_ref.at[there], recv_sem.at[there]).wait()
        return carry

    lax.fori_loop(1, devices, finish, 0)
    own.wait()


def exchanged(volts, history, taps, groups):
    devices = groups[0] * groups[1]
    taps_count, channels = taps.shape
    inputs = volts.shape[1]
    blocks = volts.shape[2] // (channels * STEP)
    planes = 2 * channels // devices
    table = dft_table(channels).reshape(2 * channels, 2 * channels)
    dtype = jnp.bfloat16
    return pl.pallas_call(
        functools.partial(exchange_kernel, groups),
        out_shape=jax.ShapeDtypeStruct((devices, blocks, planes, STEP, inputs), dtype),
        in_specs=[pl.BlockSpec(memory_space=pl.ANY)]
        + [pl.BlockSpec(memory_space=pltpu.VMEM)] * 3,
        out_specs=pl.BlockSpec(memory_space=pl.ANY),
        scratch_shapes=[
            pltpu.VMEM((2, 2, inputs, STEP * channels), dtype),
            pltpu.VMEM(history.shape, dtype),
            pltpu.VMEM((STEP * inputs, 2 * channels), dtype),
            pltpu.VMEM((2 * channels * STEP, inputs), jnp.float32),
            pltpu.VMEM((blocks, devices, planes, STEP, inputs), dtype),
            pltpu.SemaphoreType.DMA((2,)),
            pltpu.SemaphoreType.DMA((devices,)),
            pltpu.SemaphoreType.DMA((devices,)),
            pltpu.SemaphoreType.DMA,
        ],
        compiler_params=pltpu.CompilerParams(
            collective_id=0, has_side_effects=True, vmem_limit_bytes=58 * 1024 * 1024
        ),
        cost_estimate=pl.CostEstimate(
            flops=8 * channels * volts.size,
            bytes_accessed=4 * volts.size,
            transcendentals=0,
        ),
    )(volts, history, taps, table)


def correlate_kernel(groups, scale, arrived_ref, result_ref, signal, across, sems):
    time_groups, band_groups = groups
    channel = pl.program_id(0)
    count = pl.num_programs(0)
    _, blocks, _, steps, inputs = arrived_ref.shape
    total_inputs = signal.shape[4]
    length = time_groups * blocks * steps

    def load(which, slot):
        def one(there, carry):
            at_time = there // band_groups
            at_band = lax.rem(there, band_groups)
            lanes = pl.ds(pl.multiple_of(at_band * inputs, LANES), inputs)
            pltpu.make_async_copy(
                arrived_ref.at[there, :, pl.ds(which * 2, 2)],
                signal.at[slot, pl.ds(at_time * blocks, blocks), :, :, lanes],
                sems.at[slot],
            ).start()
            return carry

        lax.fori_loop(0, time_groups * band_groups, one, 0)

    slot = lax.rem(channel, 2)

    @pl.when(channel == 0)
    def _():
        load(0, 0)

    @pl.when(channel + 1 < count)
    def _():
        load(channel + 1, lax.rem(channel + 1, 2))

    pltpu.make_async_copy(signal.at[slot], signal.at[slot], sems.at[slot]).wait()

    def turn(index, carry):
        at = pl.multiple_of(index * LANES, LANES)
        for part in range(2):
            piece = signal[slot, :, part, :, pl.ds(at, LANES)].reshape(length, LANES)
            across[part, pl.ds(at, LANES), :] = piece.T
        return carry

    lax.fori_loop(0, total_inputs // LANES, turn, 0)

    def product(left, right, p, q):
        return jnp.dot(
            across[left, p, :],
            signal[slot, :, right, :, q].reshape(length, BLOCK),
            preferred_element_type=jnp.float32,
        )

    for p_at in range(0, total_inputs, BLOCK):
        p = pl.ds(p_at, BLOCK)

        def column(index, carry, p_at=p_at, p=p):
            q = pl.ds(pl.multiple_of(index * BLOCK, BLOCK), BLOCK)
            real = (product(0, 0, p, q) + product(1, 1, p, q)) * scale
            imag = (product(1, 0, p, q) - product(0, 1, p, q)) * scale
            result_ref[0, 0, p, q] = real
            result_ref[0, 1, p, q] = imag

            @pl.when(index * BLOCK > p_at)
            def _():
                result_ref[0, 0, q, p] = real.T
                result_ref[0, 1, q, p] = -imag.T

            return carry

        lax.fori_loop(p_at // BLOCK, total_inputs // BLOCK, column, 0)


def correlated(arrived, groups):
    devices, blocks, planes, steps, inputs = arrived.shape
    own = planes // 2
    total_inputs = inputs * groups[1]
    length = groups[0] * blocks * steps
    return pl.pallas_call(
        functools.partial(correlate_kernel, groups, 1.0 / length),
        grid=(own,),
        out_shape=jax.ShapeDtypeStruct((own, 2, total_inputs, total_inputs), jnp.float32),
        in_specs=[pl.BlockSpec(memory_space=pl.ANY)],
        out_specs=pl.BlockSpec((1, 2, total_inputs, total_inputs), lambda c: (c, 0, 0, 0)),
        scratch_shapes=[
            pltpu.VMEM((2, groups[0] * blocks, 2, steps, total_inputs), jnp.bfloat16),
            pltpu.VMEM((2, total_inputs, length), jnp.bfloat16),
            pltpu.SemaphoreType.DMA((2,)),
        ],
        compiler_params=pltpu.CompilerParams(vmem_limit_bytes=58 * 1024 * 1024),
        cost_estimate=pl.CostEstimate(
            flops=own * 8 * length * total_inputs * total_inputs,
            bytes_accessed=own * 12 * total_inputs * total_inputs,
            transcendentals=0,
        ),
    )(arrived)


def fits(volts, taps, groups):
    taps_count, channels = taps.shape
    frames = volts.shape[2] // channels
    return (
        volts.shape[1] == LANES
        and channels % BLOCK == 0
        and frames % STEP == 0
        and STEP >= taps_count
        and groups[1] % 2 == 0
        and volts.size * 2 <= 32 * 1024 * 1024
    )


def per_device(volts, taps):
    groups = (lax.axis_size("tm"), lax.axis_size("band"))
    if not fits(volts, taps, groups):
        return per_device_plain(volts, taps)
    margin = (taps.shape[0] - 1) * taps.shape[1]
    history = shifted(volts[:, :, volts.shape[2] - margin :], "tm", 1)
    arrived = exchanged(volts, history, taps, groups)
    return correlated(arrived, groups)


def per_device_plain(volts, taps):
    time_groups = lax.axis_size("tm")
    band_groups = lax.axis_size("band")
    taps_count = taps.shape[0]
    channels = taps.shape[1]
    local_inputs = volts.shape[1]
    samples = volts.shape[2]
    spec_local = samples // channels
    own_channels = channels // (time_groups * band_groups)
    margin = (taps_count - 1) * channels
    history = shifted(volts[:, :, samples - margin :], "tm", 1)
    frames = jnp.concatenate([history, volts], axis=2)
    frames = frames.reshape(2, local_inputs, spec_local + taps_count - 1, channels).astype(
        jnp.float32
    )
    filtered = taps[0] * frames[:, :, 0:spec_local, :]
    for weight_index in range(1, taps_count):
        filtered = (
            filtered
            + taps[weight_index] * frames[:, :, weight_index : weight_index + spec_local, :]
        )
    filtered = filtered.astype(jnp.bfloat16)
    table = dft_table(channels)
    spectra = lax.dot_general(
        table, filtered, (((1, 2), (0, 3)), ((), ())), preferred_element_type=jnp.float32
    )
    spectra = spectra.astype(jnp.bfloat16).reshape(
        time_groups, band_groups, own_channels, 2, local_inputs, spec_local
    )
    spectra_total = spec_local * time_groups
    turned = lax.all_to_all(
        lax.all_to_all(spectra, "tm", split_axis=0, concat_axis=5, tiled=True),
        "band",
        split_axis=1,
        concat_axis=4,
        tiled=True,
    )
    result = correlate(turned.reshape(own_channels, 2, turned.shape[4], spectra_total))
    return result * (1.0 / spectra_total)


def solution(mesh):
    in_specs = (P(None, "band", "tm"), P())
    out_specs = P(("tm", "band"), None, None, None)
    return jax.shard_map(
        per_device, mesh=mesh, in_specs=in_specs, out_specs=out_specs, check_vma=False
    )
```

```python
import functools
import math

import jax
import jax.numpy as jnp
from jax import lax
from jax.experimental import pallas as pl
from jax.experimental.pallas import tpu as pltpu
from jax.sharding import PartitionSpec as P


def shifted(shard, axis, by):
    size = lax.axis_size(axis)
    pairs = [(i, i + by) for i in range(size) if 0 <= i + by < size]
    return lax.ppermute(shard, axis, pairs)


def dft_table(channels):
    index = jnp.arange(channels, dtype=jnp.int32)
    turns = index[:, None] * index[None, :] % channels
    theta = turns.astype(jnp.float32) * (2.0 * math.pi / channels)
    factor = 1.0 / math.sqrt(channels)
    cosine = jnp.cos(theta) * factor
    sine = jnp.sin(theta) * factor
    real_row = jnp.stack([cosine, sine], axis=1)
    imag_row = jnp.stack([-sine, cosine], axis=1)
    table = jnp.stack([real_row, imag_row], axis=1)
    return table.reshape(2 * channels, 2, channels).astype(jnp.bfloat16)


def weighting(signal):
    swapped = jnp.stack([signal[:, 1], -signal[:, 0]], axis=1)
    return jnp.stack([signal, swapped], axis=1)


def square_products(signal):
    return jnp.einsum(
        "corps,crqs->copq", weighting(signal), signal, preferred_element_type=jnp.float32
    )


def correlate(signal):
    return square_products(signal)


STEP = 16
STRIP = 16
LANES = 128
BLOCK = 256
MESH = pl.DeviceIdType.MESH


def filter_block(volts_ref, history_ref, taps_ref, filtered_ref, steps):
    taps_count, channels = taps_ref.shape
    inputs = history_ref.shape[1]
    margin = taps_count - 1

    def strip(index, carry):
        rows = pl.ds(pl.multiple_of(index * STRIP, STRIP), STRIP)
        for part in range(2):
            for lane in range(0, channels, LANES):
                weights = [
                    jnp.broadcast_to(taps_ref[j : j + 1, lane : lane + LANES], (STRIP, LANES))
                    for j in range(taps_count)
                ]
                frames = []
                for f in range(steps + margin):
                    ref, at = (history_ref, f) if f < margin else (volts_ref, f - margin)
                    start = at * channels + lane
                    frames.append(ref[part, rows, start : start + LANES].astype(jnp.float32))
                for t in range(steps):
                    total = weights[0] * frames[t]
                    for j in range(1, taps_count):
                        total = total + weights[j] * frames[t + j]
                    out_rows = pl.ds(pl.multiple_of(t * inputs + index * STRIP, STRIP), STRIP)
                    column = part * channels + lane
                    filtered_ref[out_rows, column : column + LANES] = total.astype(jnp.bfloat16)
        return carry

    lax.fori_loop(0, inputs // STRIP, strip, 0)


def transform_block(table_ref, filtered_ref, turned_ref, steps, inputs):
    rows = table_ref.shape[0]
    for t in range(0, steps, 2):
        product = lax.dot_general(
            table_ref[...],
            filtered_ref[t * inputs : (t + 2) * inputs, :],
            (((1,), (1,)), ((), ())),
            preferred_element_type=jnp.float32,
        )
        turned_ref[pl.ds(t, rows, stride=steps), :] = product[:, :inputs]
        turned_ref[pl.ds(t + 1, rows, stride=steps), :] = product[:, inputs:]


def exchange_kernel(
    groups,
    volts_ref,
    history_in_ref,
    taps_ref,
    table_ref,
    arrived_ref,
    volts_buf,
    history,
    filtered,
    turned,
    spectra,
    in_sem,
    send_sem,
    recv_sem,
    local_sem,
):
    time_groups, band_groups = groups
    devices = time_groups * band_groups
    my_time = lax.axis_index("tm")
    my_band = lax.axis_index("band")
    me = my_time * band_groups + my_band
    blocks, _, planes, steps, inputs = spectra.shape
    channels = taps_ref.shape[1]
    width = steps * channels

    def offset(k):
        turn = lax.rem(k, band_groups)
        half = turn // 2
        parity = lax.rem(turn, 2)
        by_band = lax.rem(band_groups // 2 + half + parity * (band_groups // 2), band_groups)
        by_time = lax.rem(k // band_groups + turn, time_groups)
        return by_time, by_band

    def fetch(block):
        slot = lax.rem(block, 2)
        columns = pl.ds(pl.multiple_of(block * width, LANES), width)
        return pltpu.make_async_copy(
            volts_ref.at[:, :, columns], volts_buf.at[slot], in_sem.at[slot]
        )

    fetch(0).start()
    history[...] = history_in_ref[...]

    barrier = pltpu.get_barrier_semaphore()

    def greet(k, carry):
        there_time = lax.rem(my_time + k // band_groups, time_groups)
        there_band = lax.rem(my_band + lax.rem(k, band_groups), band_groups)
        pl.semaphore_signal(
            barrier, inc=1, device_id=(there_time, there_band), device_id_type=MESH
        )
        return carry

    lax.fori_loop(1, devices, greet, 0)
    pl.semaphore_wait(barrier, devices - 1)

    def step(block, carry):
        slot = lax.rem(block, 2)
        fetch(block).wait()

        @pl.when(block + 1 < blocks)
        def _():
            fetch(block + 1).start()

        filter_block(volts_buf.at[slot], history, taps_ref, filtered, steps)
        margin = history.shape[2]
        history[...] = volts_buf[slot, :, :, width - margin :]
        transform_block(table_ref, filtered, turned, steps, inputs)

        def pack(there, carry):
            rows = pl.ds(pl.multiple_of(there * (planes * steps), STRIP), planes * steps)
            values = turned[rows, :].reshape(planes, steps, inputs)
            spectra[block, there] = values.astype(jnp.bfloat16)
            return carry

        lax.fori_loop(0, devices, pack, 0)

        def send(k, carry):
            by_time, by_band = offset(k)
            there_time = lax.rem(my_time + by_time, time_groups)
            there_band = lax.rem(my_band + by_band, band_groups)
            there = there_time * band_groups + there_band

            @pl.when(there != me)
            def _():
                pltpu.make_async_remote_copy(
                    src_ref=spectra.at[block, there],
                    dst_ref=arrived_ref.at[me, block],
                    send_sem=send_sem.at[there],
                    recv_sem=recv_sem.at[me],
                    device_id=(there_time, there_band),
                    device_id_type=MESH,
                ).start()

            return carry

        lax.fori_loop(0, devices, send, 0)
        return carry

    lax.fori_loop(0, blocks, step, 0)
    own = pltpu.make_async_copy(spectra.at[:, me], arrived_ref.at[me], local_sem)
    own.start()

    def finish(k, carry):
        there_time = lax.rem(my_time + k // band_groups, time_groups)
        there_band = lax.rem(my_band + lax.rem(k, band_groups), band_groups)
        there = there_time * band_groups + there_band
        pltpu.make_async_copy(spectra.at[:, there], arrived_ref.at[there], send_sem.at[there]).wait()
        pltpu.make_async_copy(spectra.at[:, there], arrived_ref.at[there], recv_sem.at[there]).wait()
        return carry

    lax.fori_loop(1, devices, finish, 0)
    own.wait()


def exchanged(volts, history, taps, groups):
    devices = groups[0] * groups[1]
    taps_count, channels = taps.shape
    inputs = volts.shape[1]
    blocks = volts.shape[2] // (channels * STEP)
    planes = 2 * channels // devices
    table = dft_table(channels).reshape(2 * channels, 2 * channels)
    dtype = jnp.bfloat16
    return pl.pallas_call(
        functools.partial(exchange_kernel, groups),
        out_shape=jax.ShapeDtypeStruct((devices, blocks, planes, STEP, inputs), dtype),
        in_specs=[pl.BlockSpec(memory_space=pl.ANY)]
        + [pl.BlockSpec(memory_space=pltpu.VMEM)] * 3,
        out_specs=pl.BlockSpec(memory_space=pl.ANY),
        scratch_shapes=[
            pltpu.VMEM((2, 2, inputs, STEP * channels), dtype),
            pltpu.VMEM(history.shape, dtype),
            pltpu.VMEM((STEP * inputs, 2 * channels), dtype),
            pltpu.VMEM((2 * channels * STEP, inputs), jnp.float32),
            pltpu.VMEM((blocks, devices, planes, STEP, inputs), dtype),
            pltpu.SemaphoreType.DMA((2,)),
            pltpu.SemaphoreType.DMA((devices,)),
            pltpu.SemaphoreType.DMA((devices,)),
            pltpu.SemaphoreType.DMA,
        ],
        compiler_params=pltpu.CompilerParams(
            collective_id=0, has_side_effects=True, vmem_limit_bytes=58 * 1024 * 1024
        ),
        cost_estimate=pl.CostEstimate(
            flops=8 * channels * volts.size,
            bytes_accessed=4 * volts.size,
            transcendentals=0,
        ),
    )(volts, history, taps, table)


def correlate_kernel(groups, scale, arrived_ref, result_ref, signal, across, sems):
    time_groups, band_groups = groups
    channel = pl.program_id(0)
    count = pl.num_programs(0)
    _, blocks, _, steps, inputs = arrived_ref.shape
    total_inputs = signal.shape[4]
    length = time_groups * blocks * steps

    def load(which, slot):
        def one(there, carry):
            at_time = there // band_groups
            at_band = lax.rem(there, band_groups)
            lanes = pl.ds(pl.multiple_of(at_band * inputs, LANES), inputs)
            pltpu.make_async_copy(
                arrived_ref.at[there, :, pl.ds(which * 2, 2)],
                signal.at[slot, pl.ds(at_time * blocks, blocks), :, :, lanes],
                sems.at[slot],
            ).start()
            return carry

        lax.fori_loop(0, time_groups * band_groups, one, 0)

    slot = lax.rem(channel, 2)

    @pl.when(channel == 0)
    def _():
        load(0, 0)

    @pl.when(channel + 1 < count)
    def _():
        load(channel + 1, lax.rem(channel + 1, 2))

    pltpu.make_async_copy(signal.at[slot], signal.at[slot], sems.at[slot]).wait()

    for p_at in range(0, total_inputs, BLOCK):
        panel = p_at // BLOCK % 2
        p = slice(p_at, p_at + BLOCK)
        first = signal[slot, :, 0, :, p].reshape(length, BLOCK).T
        second = signal[slot, :, 1, :, p].reshape(length, BLOCK).T
        across[panel, 0, :, :length] = first
        across[panel, 0, :, length:] = second
        across[panel, 1, :, :length] = second
        across[panel, 1, :, length:] = -first
        for q_at in range(p_at, total_inputs, BLOCK):
            q = slice(q_at, q_at + BLOCK)
            down = jnp.concatenate(
                [signal[slot, :, part, :, q].reshape(length, BLOCK) for part in range(2)], axis=0
            )
            product = scale * jnp.dot(
                across[panel].reshape(2 * BLOCK, 2 * length),
                down,
                preferred_element_type=jnp.float32,
            )
            real, imag = product[:BLOCK], product[BLOCK:]
            result_ref[0, 0, p, q] = real
            result_ref[0, 1, p, q] = imag
            if q_at > p_at:
                result_ref[0, 0, q, p] = real.T
                result_ref[0, 1, q, p] = -imag.T


def correlated(arrived, groups):
    devices, blocks, planes, steps, inputs = arrived.shape
    own = planes // 2
    total_inputs = inputs * groups[1]
    length = groups[0] * blocks * steps
    return pl.pallas_call(
        functools.partial(correlate_kernel, groups, 1.0 / length),
        grid=(own,),
        out_shape=jax.ShapeDtypeStruct((own, 2, total_inputs, total_inputs), jnp.float32),
        in_specs=[pl.BlockSpec(memory_space=pl.ANY)],
        out_specs=pl.BlockSpec((1, 2, total_inputs, total_inputs), lambda c: (c, 0, 0, 0)),
        scratch_shapes=[
            pltpu.VMEM((2, groups[0] * blocks, 2, steps, total_inputs), jnp.bfloat16),
            pltpu.VMEM((2, 2, BLOCK, 2 * length), jnp.bfloat16),
            pltpu.SemaphoreType.DMA((2,)),
        ],
        compiler_params=pltpu.CompilerParams(vmem_limit_bytes=58 * 1024 * 1024),
        cost_estimate=pl.CostEstimate(
            flops=own * 8 * length * total_inputs * total_inputs,
            bytes_accessed=own * 12 * total_inputs * total_inputs,
            transcendentals=0,
        ),
    )(arrived)


def fits(volts, taps, groups):
    taps_count, channels = taps.shape
    frames = volts.shape[2] // channels
    return (
        volts.shape[1] == LANES
        and channels % BLOCK == 0
        and frames % STEP == 0
        and STEP >= taps_count
        and groups[1] % 2 == 0
        and volts.size * 2 <= 32 * 1024 * 1024
    )


def per_device(volts, taps):
    groups = (lax.axis_size("tm"), lax.axis_size("band"))
    if not fits(volts, taps, groups):
        return per_device_plain(volts, taps)
    margin = (taps.shape[0] - 1) * taps.shape[1]
    history = shifted(volts[:, :, volts.shape[2] - margin :], "tm", 1)
    arrived = exchanged(volts, history, taps, groups)
    return correlated(arrived, groups)


def per_device_plain(volts, taps):
    time_groups = lax.axis_size("tm")
    band_groups = lax.axis_size("band")
    taps_count = taps.shape[0]
    channels = taps.shape[1]
    local_inputs = volts.shape[1]
    samples = volts.shape[2]
    spec_local = samples // channels
    own_channels = channels // (time_groups * band_groups)
    margin = (taps_count - 1) * channels
    history = shifted(volts[:, :, samples - margin :], "tm", 1)
    frames = jnp.concatenate([history, volts], axis=2)
    frames = frames.reshape(2, local_inputs, spec_local + taps_count - 1, channels).astype(
        jnp.float32
    )
    filtered = taps[0] * frames[:, :, 0:spec_local, :]
    for weight_index in range(1, taps_count):
        filtered = (
            filtered
            + taps[weight_index] * frames[:, :, weight_index : weight_index + spec_local, :]
        )
    filtered = filtered.astype(jnp.bfloat16)
    table = dft_table(channels)
    spectra = lax.dot_general(
        table, filtered, (((1, 2), (0, 3)), ((), ())), preferred_element_type=jnp.float32
    )
    spectra = spectra.astype(jnp.bfloat16).reshape(
        time_groups, band_groups, own_channels, 2, local_inputs, spec_local
    )
    spectra_total = spec_local * time_groups
    turned = lax.all_to_all(
        lax.all_to_all(spectra, "tm", split_axis=0, concat_axis=5, tiled=True),
        "band",
        split_axis=1,
        concat_axis=4,
        tiled=True,
    )
    result = correlate(turned.reshape(own_channels, 2, turned.shape[4], spectra_total))
    return result * (1.0 / spectra_total)


def solution(mesh):
    in_specs = (P(None, "band", "tm"), P())
    out_specs = P(("tm", "band"), None, None, None)
    return jax.shard_map(
        per_device, mesh=mesh, in_specs=in_specs, out_specs=out_specs, check_vma=False
    )
```
